128 devices in a mesh: gy: 16 (over x_hi, z, core), gx: 4 (over y), tp: 2 (over x_lo).
Axes of the slice: x: 4 (x_hi: 2, x_lo: 2; x = x_hi * 2 + x_lo), y: 4, z: 4, core: 2. Of those that a mesh axis runs over, the one named last changes fastest.
Arguments:
- features: float32 [4, 256, 64, 1536], P(None, 'gy', 'gx')
- qkv_weight: bfloat16 [2, 1536, 3, 1536], P(None, None, None, 'tp')
- out_weight: bfloat16 [2, 1536, 1536], P(None, 'tp'), may hold values from -0.15625 to 0.15625
- norm_gain: float32 [2, 1536], replicated, may hold values from 0.5 to 1.5
- layer_scale: float32 [2, 1536], replicated, may hold values from 0.5 to 2
- valid_counts: int32 [16, 4], replicated, may hold values from 137 to 256, as said below
Outputs:
- blended: float32 [4, 256, 64, 1536], P(None, 'gy', 'gx')
The draws below stay inside these ranges and needn't reach their ends.
Inputs may be any that keep to these rules, and one draw needn't show every extreme that they name: `valid_counts`: every tile is valid from its first patch in row-major order up to its count; some tile is complete.
All inputs are finite; a program needn't handle non-finite values.
Results may differ from the reference program's by a relative error of at most 0.009.
Values may be sent and summed in bfloat16 or wider, within the bound.
A program may use at most 128 MiB of HBM per device.

```python
import math
import jax
import jax.numpy as jnp
from jax import lax

D = 1536
HD = 64
LAYERS = 2
TH = 16
TW = 16
IMGS = 4
NROWS = 256
NCOLS = 64
GRID_ROWS = 16
GRID_COLS = 4
N_GY = 16
N_GX = 4
N_TP = 2


def draw_features(key, part):
    key = jax.random.fold_in(key, 5)
    first_key = jax.random.fold_in(key, 0)
    full_shape = (IMGS, NROWS, NCOLS, D)
    values = jax.random.truncated_normal(first_key, -6.0, 6.0, full_shape)
    return values.astype(jnp.float32)


def draw_qkv_weight(key, part):
    key = jax.random.fold_in(key, 11)
    first_key = jax.random.fold_in(key, 0)
    base = jax.random.truncated_normal(first_key, -3.0, 3.0, (LAYERS, D, 3, D)) * D ** (-0.5)
    values = base
    return values.astype(jnp.float32).astype(jnp.bfloat16)


def draw_valid_counts(key, part):
    key = jax.random.fold_in(key, 9)
    first_key, second_key = jax.random.split(key, 2)
    lowest = TH * TW // 2 + TW // 2 + 1
    counts = jax.random.randint(first_key, (GRID_ROWS, GRID_COLS), lowest, TH * TW + 1)
    chosen = jax.random.randint(second_key, (), 0, GRID_ROWS * GRID_COLS)
    flat_index = jnp.arange(GRID_ROWS * GRID_COLS).reshape(GRID_ROWS, GRID_COLS)
    return jnp.where(flat_index == chosen, TH * TW, counts).astype(jnp.int32)


def level_of(stream_key, extent, shards, smallest, high):
    gain = 1.0
    for dim, parts in shards:
        draws = jax.random.uniform(jax.random.fold_in(jax.random.fold_in(stream_key, 6), dim), (parts,), jnp.float32, smallest / len(shards), high / len(shards))
        gain = gain * jnp.repeat(jnp.exp(draws), extent[dim] // parts).reshape((-1,) + (1,) * (len(extent) - 1 - dim))
    return gain


def normal_values(stream_key, extent, width, most, cuts=(), kind=jnp.bfloat16):
    array = width * jax.random.normal(stream_key, extent, jnp.float32)
    if cuts:
        array = array * level_of(stream_key, extent, cuts, -0.22, 0.18)
    return jnp.clip(array, -most, most).astype(kind)


def setup_inputs(seed: int = 0) -> dict:
    splits = jax.random.split(jax.random.key(seed), 7)
    return {
        "features": draw_features(jax.random.fold_in(splits[6], 71), 0),
        "qkv_weight": draw_qkv_weight(jax.random.fold_in(splits[6], 71), 0),
        "out_weight": normal_values(splits[2], (LAYERS, D, D), D ** -0.5, 0.15625, ((1, 2),)),
        "norm_gain": jnp.clip(1.0 + 0.1 * jax.random.normal(splits[3], (LAYERS, D), jnp.float32), 0.5, 1.5),
        "layer_scale": jnp.clip(jnp.exp(jax.random.uniform(splits[4], (LAYERS, D), jnp.float32, math.log(0.5), math.log(2.0))), 0.5, 2.0),
        "valid_counts": draw_valid_counts(jax.random.fold_in(splits[6], 71), 0),
    }


def normalize(values, gain_row):
    average = lax.optimization_barrier(jnp.mean(values, axis=-1, keepdims=True))
    centred = values - average
    spread = lax.optimization_barrier(jnp.mean(centred * centred, axis=-1, keepdims=True))
    return (centred * lax.rsqrt(spread + 1e-06) * gain_row).astype(jnp.bfloat16)

def attend(normed, valid, qkv_w):
    length, channels = normed.shape
    inner = qkv_w.shape[-1]
    packed = jnp.dot(normed, qkv_w.reshape(channels, -1), preferred_element_type=jnp.float32).astype(jnp.bfloat16)
    packed = packed.reshape(length, 3, inner // HD, HD)
    query_part = packed[:, 0].astype(jnp.float32)
    key_part = packed[:, 1].astype(jnp.float32)
    value_part = packed[:, 2].astype(jnp.float32)
    scores = jnp.einsum('qhe,khe->hqk', query_part, key_part) * HD ** (-0.5)
    scores = jnp.where(valid[None, None, :], scores, -1e+30)
    largest = lax.optimization_barrier(jnp.max(scores, axis=-1, keepdims=True))
    powers = jnp.exp(scores - largest)
    totals = lax.optimization_barrier(jnp.sum(powers, axis=-1, keepdims=True))
    attn_prob = (powers / totals).astype(jnp.bfloat16).astype(jnp.float32)
    head_out = jnp.einsum('hqk,khe->qhe', attn_prob, value_part)
    return head_out.reshape(length, inner).astype(jnp.bfloat16)

def project_sum(head_out, proj):
    inner = head_out.shape[-1] // N_TP
    flat = head_out.reshape(-1, head_out.shape[-1])
    total = jnp.zeros((flat.shape[0], proj.shape[1]), jnp.float32)
    for member in range(N_TP):
        part_out = jnp.dot(flat[:, member * inner:(member + 1) * inner], proj[member * inner:(member + 1) * inner], preferred_element_type=jnp.float32)
        rounded = lax.optimization_barrier(part_out.astype(jnp.bfloat16))
        total = total + rounded.astype(jnp.float32)
    return total.reshape(head_out.shape[:-1] + (proj.shape[1],))

def tile_layer(normed_full, valid_full, qkv_w, proj):
    images = normed_full.shape[0]
    tiles = normed_full.reshape(images, N_GY, TH, N_GX, TW, D).transpose(1, 3, 0, 2, 4, 5).reshape(N_GY, N_GX, images, TH * TW, D)
    masks = valid_full.reshape(N_GY, TH, N_GX, TW).transpose(0, 2, 1, 3).reshape(N_GY, N_GX, TH * TW)

    def grid_row(packed_row):
        tile_row, mask_row = packed_row
        per_image = jax.vmap(attend, in_axes=(0, None, None))
        head_out = jax.vmap(per_image, in_axes=(0, 0, None))(tile_row, mask_row, qkv_w)
        return project_sum(head_out, proj)
    summed = lax.map(grid_row, (tiles, masks))
    return summed.reshape(N_GY, N_GX, images, TH, TW, D).transpose(2, 0, 3, 1, 4, 5).reshape(images, NROWS, NCOLS, D)

def blend_weight(tile_rows, tile_cols):
    row_part = jnp.sin(jnp.pi * (jnp.arange(tile_rows, dtype=jnp.float32) + 0.5) / tile_rows) ** 2
    col_part = jnp.sin(jnp.pi * (jnp.arange(tile_cols, dtype=jnp.float32) + 0.5) / tile_cols) ** 2
    return (0.25 + 0.75 * row_part[:, None] * col_part[None, :])[:, :, None]

def reference(features, qkv_weight, out_weight, norm_gain, layer_scale, valid_counts):
    row_index = jnp.arange(NROWS, dtype=jnp.int32)[:, None]
    col_index = jnp.arange(NCOLS, dtype=jnp.int32)[None, :]
    tile_count = jnp.repeat(jnp.repeat(valid_counts, TH, axis=0), TW, axis=1)
    valid_full = row_index % TH * TW + col_index % TW < tile_count
    normed = normalize(features, norm_gain[0])
    summed = tile_layer(normed, valid_full, qkv_weight[0], out_weight[0])
    after_first = features + layer_scale[0] * summed
    normed = normalize(after_first, norm_gain[1])
    shifted = jnp.pad(normed, ((0, 0), (0, TH // 2), (0, TW // 2), (0, 0)))[:, TH // 2:, TW // 2:]
    valid_shift = jnp.pad(valid_full, ((0, TH // 2), (0, TW // 2)))[TH // 2:, TW // 2:]
    summed = tile_layer(shifted, valid_shift, qkv_weight[1], out_weight[1])
    blend_map = jnp.tile(blend_weight(TH, TW), (N_GY, N_GX, 1))
    change = layer_scale[1] * blend_map * summed
    placed = jnp.pad(change, ((0, 0), (TH // 2, 0), (TW // 2, 0), (0, 0)))[:, :NROWS, :NCOLS]
    return after_first + placed
```

```python
import functools

import jax
import jax.numpy as jnp
import numpy as np
from jax import lax
from jax.experimental import pallas as pl
from jax.experimental.pallas import tpu as pltpu
from jax.sharding import PartitionSpec as P

F32 = jnp.float32
BF = jnp.bfloat16
MESH = pl.DeviceIdType.MESH
HD = 64
GROUP = 4
SCALE = HD**-0.5 * 1.4426950408889634
STAGES = (("o", 0), ("q", 0), ("q", 1), ("q", 2), ("o", 1))


def layer_norm(v, gain):
    centred = v - jnp.mean(v, axis=-1, keepdims=True)
    spread = jnp.mean(centred * centred, axis=-1, keepdims=True)
    return (centred * lax.rsqrt(spread + 1e-06) * gain).astype(BF)


def attend(q, k, v, bias):
    rows = q.shape[0]
    lane = lax.broadcasted_iota(jnp.int32, (rows, 4 * HD), 1)
    low = lax.broadcasted_iota(jnp.int32, (rows, 2 * HD), 1) < HD
    keys = k.T
    none = jnp.zeros((HD, rows), BF)
    keys = jnp.concatenate(
        [
            jnp.concatenate([keys[HD * h : HD * h + HD] if g == h else none for g in range(GROUP)], axis=0)
            for h in range(GROUP)
        ],
        axis=1,
    )
    scores = jnp.dot(q, keys, preferred_element_type=F32)
    powers, scale = [], []
    for h in range(GROUP):
        s = scores[:, rows * h : rows * h + rows] * SCALE + bias
        e = jnp.exp2(s - jnp.max(s, axis=-1, keepdims=True))
        powers.append(e.astype(BF))
        scale.append(1.0 / jnp.sum(e, axis=-1, keepdims=True))
    empty = jnp.zeros((rows, 4 * HD), BF)
    values = jnp.concatenate(
        [jnp.where((lane >= HD * h) & (lane < HD * h + HD), v, empty) for h in range(GROUP)], axis=0
    )
    out = jnp.dot(jnp.concatenate(powers, axis=1), values, preferred_element_type=F32)
    left = out[:, : 2 * HD] * jnp.where(low, scale[0], scale[1])
    right = out[:, 2 * HD :] * jnp.where(low, scale[2], scale[3])
    return jnp.concatenate([left.astype(BF), right.astype(BF)], axis=1)


def kernel(
    counts, feats, wq_hbm, wo_hbm, gain, lscale, blend, out,
    wq, wo_own, wo_oth, x, nin, crop, qkv, heads, heads_in, heads2,
    upd_out, upd_in, fin_out, fin_in, bias,
    s_feat, s_wq, s_wo, s_out, h_send, h_recv, c_send, c_recv, u_send, u_recv, f_send, f_recv,
    x_send, x_recv, n_send, n_recv, b_send, b_recv,
):
    gy, gx, tp = lax.axis_index("gy"), lax.axis_index("gx"), lax.axis_index("tp")
    core, z, x_hi = gy % 2, (gy // 2) % 4, gy // 8
    dim = feats.shape[-1]
    tok = 256
    half = wo_hbm.shape[1]
    ng = half // 256

    def at_z(step):
        return (x_hi * 8 + ((z + step) % 4) * 2 + core, gx, tp)

    def at_y(step):
        return (gy, (gx + step) % 4, tp)

    twin = (gy + 1 - 2 * core, gx, tp)
    mate = (gy, gx, 1 - tp)
    mate_b = ((gy + 8) % 16, gx, 1 - tp)

    def remote(src, dst, ss, rs, dev):
        return pltpu.make_async_remote_copy(
            src_ref=src, dst_ref=dst, send_sem=ss, recv_sem=rs, device_id=dev, device_id_type=MESH
        )

    images = [3 * (1 - tp), 3 * tp, 1, 2]

    def quad(ref, image, t):
        return ref.at[image, pl.ds(8 * (t % 2), 8), pl.ds(8 * (t // 2), 8), :]

    def feat_copy(slot, t):
        return pltpu.make_async_copy(quad(feats, images[slot], t), x.at[slot, t], s_feat.at[slot, t])

    def out_copy(slot, t):
        return pltpu.make_async_copy(x.at[slot, t], quad(out, images[slot], t), s_out.at[slot, t])

    def wq_copy(layer, g):
        i = ng * layer + g
        return pltpu.make_async_copy(wq_hbm.at[layer, :, :, pl.ds(256 * g, 256)], wq.at[i], s_wq.at[i])

    def wo_copy(layer):
        return pltpu.make_async_copy(wo_hbm.at[layer], wo_own.at[layer], s_wo.at[layer])

    for t in range(4):
        feat_copy(0, t).start()
    for g in range(ng):
        wq_copy(0, g).start()

    barrier = pltpu.get_barrier_semaphore()

    def greet(dev):
        pl.semaphore_signal(barrier, inc=1, device_id=dev, device_id_type=MESH)

    for dev in (mate, mate_b, twin, at_z(1), at_z(-1), at_y(1), at_y(-1)):
        greet(dev)

    @pl.when(gy > 0)
    def _():
        greet((gy - 1, gx, tp))
        greet((gy - 1, (gx + 3) % 4, tp))

    @pl.when(gy < 15)
    def _():
        greet((gy + 1, gx, tp))
        greet((gy + 1, (gx + 1) % 4, tp))

    token = lax.broadcasted_iota(jnp.int32, (8, tok), 1)
    t_of, rr, cc = token // 64, (token % 64) // 8, token % 8

    def place(t):
        return (8 * (t % 2) + rr) * 16 + 8 * (t // 2) + cc

    bias[0] = jnp.where(place(t_of) < counts[gx, gy], 0.0, -1e30)
    below, right = jnp.minimum(gy + 1, 15), jnp.minimum(gx + 1, 3)
    in_y, in_x = gy < 15, gx < 3
    limit = jnp.full((8, tok), counts[gx, gy], jnp.int32)
    limit = jnp.where(t_of == 1, jnp.where(in_y, counts[gx, below], 0), limit)
    limit = jnp.where(t_of == 2, jnp.where(in_x, counts[right, gy], 0), limit)
    limit = jnp.where(t_of == 3, jnp.where(in_y & in_x, counts[right, below], 0), limit)
    bias[1] = jnp.where(place(3 - t_of) < limit, 0.0, -1e30)

    for slot in range(1, 4):
        for t in range(4):
            feat_copy(slot, t).start()
    wo_copy(0).start()

    @pl.when(gy == 0)
    def _():
        for k in range(3):
            upd_in[k, 0] = jnp.zeros((64, dim), BF)
            upd_in[k, 2] = jnp.zeros((64, dim), BF)

    @pl.when(gy == 15)
    def _():
        for k in range(3):
            crop[k, 64:128] = jnp.zeros((64, dim), BF)
            crop[k, 192:256] = jnp.zeros((64, dim), BF)

    pl.semaphore_wait(barrier, 7 + jnp.where(gy > 0, 2, 0) + jnp.where(gy < 15, 2, 0))

    def piece(s, col, part, rows_of):
        kind, idx = STAGES[s]
        depth = dim if kind == "q" else half
        per = depth // 8
        base = (col % 4) * (2 * per) + core * per
        size = per
        if part is not None:
            size = per // 2
            base = base + part * size
        rows = pl.ds(pl.multiple_of(base, 16), size)
        if kind == "q":
            if rows_of == "src":
                return wq_hbm.at[1, :, rows, pl.ds(256 * idx, 256)]
            return wq.at[2 * ng + idx, :, rows, :]
        if rows_of == "src":
            return wo_hbm.at[idx, rows, :]
        return wo_oth.at[idx, rows, :]

    def along_y(s):
        return s % 2 == 0

    def colour(s):
        return (gx + 2 * z) % 4 if along_y(s) else (z + 2 * gx) % 4

    def x_copies(s):
        col = colour(s)
        if s == 0:
            return [
                remote(piece(s, col, i, "src"), piece(s, col, i, "dst"), x_send.at[s, i], x_recv.at[s, i], dev)
                for i, dev in enumerate((mate, mate_b))
            ]
        return [remote(piece(s, col, None, "src"), piece(s, col, None, "dst"), x_send.at[s, 1], x_recv.at[s, 1], mate_b)]

    def n_copies(s, arriving=False):
        col = colour(s)
        near, far = (at_y, at_z) if along_y(s) else (at_z, at_y)
        plan = ((near(1), None, col - 1), (near(-1), None, col + 1), (far(1), 0, col + 2), (far(-1), 1, col + 2))
        res = []
        for i, (dev, part, other) in enumerate(plan):
            ref = piece(s, (other + 4) if arriving else col, part, "dst")
            res.append(remote(ref, ref, n_send.at[s, i], n_recv.at[s, i], dev))
        return res

    def b_copy(s, i):
        col = colour(s) + (0, 3, 1, 2)[i]
        ref = piece(s, col, None, "dst")
        return remote(ref, ref, b_send.at[s, i], b_recv.at[s, i], twin)

    def b_arrival(s, i):
        kind, idx = STAGES[s]
        depth = dim if kind == "q" else half
        per = depth // 8
        col = colour(s) + (0, 3, 1, 2)[i]
        rows = pl.ds(pl.multiple_of((col % 4) * (2 * per) + (1 - core) * per, 16), per)
        ref = wq.at[2 * ng + idx, :, rows, :] if kind == "q" else wo_oth.at[idx, rows, :]
        return remote(ref, ref, b_send.at[s, i], b_recv.at[s, i], twin)

    def first_hop(s):
        for c in x_copies(s):
            c.start()

    def second_hop(s):
        for c in x_copies(s):
            c.wait_recv()
        for c in n_copies(s):
            c.start()
        b_copy(s, 0).start()
        if s + 2 < len(STAGES):
            first_hop(s + 2)

    def third_hop(s):
        for c in n_copies(s, arriving=True):
            c.wait_recv()
        for i in (1, 2, 3):
            b_copy(s, i).start()

    def arrived(s):
        for i in range(4):
            b_arrival(s, i).wait_recv()

    first_hop(0)
    first_hop(1)
    for g in range(ng):
        wq_copy(1, g).start()
    wo_copy(1).start()

    def norm_into(slot, layer):
        for t in range(4):
            nin[slot, 64 * t : 64 * t + 64] = layer_norm(x[slot, t].reshape(64, dim), gain[layer : layer + 1, :])

    def project_in(n, w):
        return [jnp.dot(n, wq[w, j], preferred_element_type=F32).astype(BF) for j in range(3)]

    def keep(parts):
        for j in range(3):
            qkv[j] = parts[j]

    def heads_copy(idx, g):
        job = jnp.where(idx == 0, 0, idx + 1)
        return remote(heads.at[job, g], heads_in.at[idx, g], h_send.at[idx, g], h_recv.at[idx, g], mate)

    def feats_ready(slot):
        for t in range(4):
            feat_copy(slot, t).wait()

    feats_ready(0)
    norm_into(0, 0)
    for g in range(ng):
        wq_copy(0, g).wait()
    for slot in range(1, 4):
        feats_ready(slot)
    keep(project_in(nin[0], 0))

    steps = 4 * ng

    def first_step(i, carry):
        job, g = i // ng, i % ng

        @pl.when((g == 0) & (job < 3))
        def _():
            norm_into(job + 1, 0)

        later = jnp.minimum(i + 1, steps - 1)
        parts = project_in(nin[later // ng], later % ng)
        heads[job, g] = attend(qkv[0], qkv[1], qkv[2], bias[0, 0:1, :])
        keep(parts)

        @pl.when(job != 1)
        def _():
            heads_copy(jnp.where(job == 0, 0, job - 1), g).start()

        @pl.when(i == 2)
        def _():
            second_hop(0)

        @pl.when(i == 8)
        def _():
            third_hop(0)

        @pl.when(i == 9)
        def _():
            second_hop(1)

        return carry

    lax.fori_loop(0, steps, first_step, 0)

    def crop_copy(k, p):
        dev = (gy - (p % 2), (gx + 4 - p // 2) % 4, tp)
        return remote(
            nin.at[k + 1, pl.ds(64 * (3 - p), 64), :], crop.at[k, pl.ds(64 * p, 64), :],
            c_send.at[k, p - 1], c_recv.at[k, p - 1], dev,
        )

    def finish_first(k):
        for g in range(ng):
            heads_copy(k, g).wait_recv()
        own = jnp.concatenate([heads[k + 1, g] for g in range(ng)], axis=1)
        oth = jnp.concatenate([heads_in[k, g] for g in range(ng)], axis=1)

        def chunk(c, carry):
            cols = pl.ds(pl.multiple_of(c * 512, 512), 512)
            acc = jnp.dot(own, wo_own[0, :, cols], preferred_element_type=F32)
            acc = acc + jnp.dot(oth, wo_oth[0, :, cols], preferred_element_type=F32)
            acc = acc * lscale[0:1, cols]
            x[k + 1, :, :, :, cols] += acc.reshape(4, 8, 8, 512)
            if k == 0:
                fin_out[:, cols] = acc.astype(BF)
            return carry

        lax.fori_loop(0, dim // 512, chunk, 0)
        norm_into(k + 1, 1)
        crop_copy(k, 2).start()

        @pl.when(gy > 0)
        def _():
            crop_copy(k, 3).start()
            crop_copy(k, 1).start()

        crop[k, 0:64] = nin[k + 1, 192:256]

    wo_copy(0).wait()
    arrived(0)
    finish_first(0)
    third_hop(1)
    second_hop(2)
    finish_first(1)
    for g in range(ng):
        wq_copy(1, g).wait()
    wo_copy(1).wait()
    third_hop(2)
    second_hop(3)

    def upd_copy(k, p):
        dev = (gy + (p % 2), (gx + p // 2) % 4, tp)
        return remote(upd_out.at[k, p - 1], upd_in.at[k, 3 - p], u_send.at[k, p - 1], u_recv.at[k, p - 1], dev)

    def fin_copy(t):
        return remote(fin_out.at[pl.ds(64 * t, 64), :], fin_in.at[t], f_send.at[t], f_recv.at[t], mate)

    def crop_ready(k):
        crop_copy(k, 2).wait_recv()

        @pl.when(gy < 15)
        def _():
            crop_copy(k, 1).wait_recv()
            crop_copy(k, 3).wait_recv()

    def attend_crop(k):
        crop_ready(k)
        keep(project_in(crop[k], ng))

        def step(g, carry):
            if k == 0:

                @pl.when(g == 2)
                def _():
                    arrived(1)
                    finish_first(2)
                    third_hop(3)
                    second_hop(4)

                @pl.when(g == 3)
                def _():
                    arrived(2)

                @pl.when(g == 4)
                def _():
                    arrived(3)

            parts = project_in(crop[k], ng + g + 1)
            heads2[g] = attend(qkv[0], qkv[1], qkv[2], bias[1, 0:1, :])
            keep(parts)
            return carry

        lax.fori_loop(0, 2 * ng - 1, step, 0)
        heads2[2 * ng - 1] = attend(qkv[0], qkv[1], qkv[2], bias[1, 0:1, :])

    def project_crop(k):
        for lo in (128, 0):
            own = jnp.concatenate([heads2[g, lo : lo + 128] for g in range(ng)], axis=1)
            oth = jnp.concatenate([heads2[ng + g, lo : lo + 128] for g in range(ng)], axis=1)

            def chunk(c, carry, lo=lo, own=own, oth=oth):
                cols = pl.ds(pl.multiple_of(c * 512, 512), 512)
                acc = jnp.dot(own, wo_own[1, :, cols], preferred_element_type=F32)
                acc = acc + jnp.dot(oth, wo_oth[1, :, cols], preferred_element_type=F32)
                weight = jnp.concatenate([blend[lo : lo + 128]] * 4, axis=1)
                acc = acc * (lscale[1:2, cols] * weight)
                if lo == 0:
                    x[k + 1, 3, :, :, cols] += acc[:64].reshape(8, 8, 512)
                    upd_out[k, 0, :, cols] = acc[64:].astype(BF)
                    if k == 0:
                        fin_out[192:256, cols] = (fin_out[192:256, cols].astype(F32) + acc[:64]).astype(BF)
                else:
                    upd_out[k, 1, :, cols] = acc[:64].astype(BF)
                    upd_out[k, 2, :, cols] = acc[64:].astype(BF)
                return carry

            lax.fori_loop(0, dim // 512, chunk, 0)
            if lo == 128:
                upd_copy(k, 2).start()

                @pl.when(gy < 15)
                def _():
                    upd_copy(k, 3).start()
            else:

                @pl.when(gy < 15)
                def _():
                    upd_copy(k, 1).start()

                out_copy(k + 1, 3).start()
                if k == 0:
                    fin_copy(3).start()

    def blend_in(k):
        upd_copy(k, 2).wait_recv()

        @pl.when(gy > 0)
        def _():
            upd_copy(k, 1).wait_recv()
            upd_copy(k, 3).wait_recv()

        for t in (0, 1, 2):
            come = upd_in[k, t].astype(F32)
            if t < 2:
                come = jnp.where(gx > 0, come, 0.0)
            x[k + 1, t] += come.reshape(8, 8, dim)
            if k == 0:
                rows = slice(64 * t, 64 * t + 64)
                fin_out[rows] = (fin_out[rows].astype(F32) + come).astype(BF)
                fin_copy(t).start()
            out_copy(k + 1, t).start()

    attend_crop(0)
    third_hop(4)
    arrived(4)
    project_crop(0)
    attend_crop(1)
    project_crop(1)
    blend_in(0)
    attend_crop(2)
    project_crop(2)
    blend_in(1)
    for t in (3, 0, 1, 2):
        fin_copy(t).wait_recv()
        x[0, t] += fin_in[t].astype(F32).reshape(8, 8, dim)
        out_copy(0, t).start()
    blend_in(2)

    for s in range(len(STAGES)):
        for c in x_copies(s):
            c.wait_send()
        for c in n_copies(s):
            c.wait_send()
        for i in range(4):
            b_copy(s, i).wait_send()
    for k in range(3):
        for g in range(ng):
            heads_copy(k, g).wait_send()
        crop_copy(k, 2).wait_send()
        upd_copy(k, 2).wait_send()

        @pl.when(gy > 0)
        def _():
            crop_copy(k, 1).wait_send()
            crop_copy(k, 3).wait_send()

        @pl.when(gy < 15)
        def _():
            upd_copy(k, 1).wait_send()
            upd_copy(k, 3).wait_send()

    for t in range(4):
        fin_copy(t).wait_send()
        for slot in range(4):
            out_copy(slot, t).wait()


def blend_rows():
    token = np.arange(256)
    t, rr, cc = token // 64, (token % 64) // 8, token % 8
    r, c = 8 * (t % 2) + rr, 8 * (t // 2) + cc
    row = np.sin(np.pi * (r.astype(np.float32) + 0.5) / 16) ** 2
    col = np.sin(np.pi * (c.astype(np.float32) + 0.5) / 16) ** 2
    weight = (0.25 + 0.75 * row * col).astype(np.float32)
    return np.broadcast_to(weight[:, None], (256, 128)).copy()


def shards(features, qkv_weight, out_weight, norm_gain, layer_scale, valid_counts):
    dim = features.shape[-1]
    half = out_weight.shape[1]
    ng = half // 256
    anywhere = pl.BlockSpec(memory_space=pl.ANY)
    vmem = pl.BlockSpec(memory_space=pltpu.VMEM)
    dma = pltpu.SemaphoreType.DMA
    ns = len(STAGES)
    return pl.pallas_call(
        kernel,
        out_shape=jax.ShapeDtypeStruct(features.shape, F32),
        in_specs=[pl.BlockSpec(memory_space=pltpu.SMEM), anywhere, anywhere, anywhere, vmem, vmem, vmem],
        out_specs=anywhere,
        scratch_shapes=[
            pltpu.VMEM((3 * ng, 3, dim, 256), BF),
            pltpu.VMEM((2, half, dim), BF),
            pltpu.VMEM((2, half, dim), BF),
            pltpu.VMEM((4, 4, 8, 8, dim), F32),
            pltpu.VMEM((4, 256, dim), BF),
            pltpu.VMEM((3, 256, dim), BF),
            pltpu.VMEM((3, 256, 256), BF),
            pltpu.VMEM((4, ng, 256, 256), BF),
            pltpu.VMEM((3, ng, 256, 256), BF),
            pltpu.VMEM((2 * ng, 256, 256), BF),
            pltpu.VMEM((3, 3, 64, dim), BF),
            pltpu.VMEM((3, 3, 64, dim), BF),
            pltpu.VMEM((256, dim), BF),
            pltpu.VMEM((4, 64, dim), BF),
            pltpu.VMEM((2, 8, 256), F32),
            dma((4, 4)), dma((2 * ng,)), dma((2,)), dma((4, 4)),
            dma((3, ng)), dma((3, ng)), dma((3, 3)), dma((3, 3)), dma((3, 3)), dma((3, 3)), dma((4,)), dma((4,)),
            dma((ns, 2)), dma((ns, 2)), dma((ns, 4)), dma((ns, 4)), dma((ns, 4)), dma((ns, 4)),
        ],
        compiler_params=pltpu.CompilerParams(
            collective_id=0, has_side_effects=True, vmem_limit_bytes=60 * 2**20
        ),
        name="two_sublayers",
    )(
        valid_counts.T, features, jnp.transpose(qkv_weight, (0, 2, 1, 3)), out_weight,
        norm_gain, layer_scale, jnp.asarray(blend_rows()),
    )


def solution(mesh):
    in_specs = (
        P(None, "gy", "gx", None),
        P(None, None, None, "tp"),
        P(None, "tp", None),
        P(),
        P(),
        P(),
    )
    out_specs = P(None, "gy", "gx", None)
    return jax.shard_map(shards, mesh=mesh, in_specs=in_specs, out_specs=out_specs, check_vma=False)
```

```python
import functools

import jax
import jax.numpy as jnp
import numpy as np
from jax import lax
from jax.experimental import pallas as pl
from jax.experimental.pallas import tpu as pltpu
from jax.sharding import PartitionSpec as P

F32 = jnp.float32
BF = jnp.bfloat16
MESH = pl.DeviceIdType.MESH
HD = 64
GROUP = 4
SCALE = HD**-0.5 * 1.4426950408889634
STAGES = (("o", 0), ("q", 0), ("q", 1), ("q", 2), ("o", 1))


def layer_norm(v, gain):
    centred = v - jnp.mean(v, axis=-1, keepdims=True)
    spread = jnp.mean(centred * centred, axis=-1, keepdims=True)
    return (centred * lax.rsqrt(spread + 1e-06) * gain).astype(BF)


def attend(q, k, v, bias):
    rows = q.shape[0]
    lane = lax.broadcasted_iota(jnp.int32, (rows, 4 * HD), 1)
    low = lax.broadcasted_iota(jnp.int32, (rows, 2 * HD), 1) < HD
    keys = k.T
    none = jnp.zeros((HD, rows), BF)
    keys = jnp.concatenate(
        [
            jnp.concatenate([keys[HD * h : HD * h + HD] if g == h else none for g in range(GROUP)], axis=0)
            for h in range(GROUP)
        ],
        axis=1,
    )
    scores = jnp.dot(q, keys, preferred_element_type=F32)
    powers, scale = [], []
    for h in range(GROUP):
        s = scores[:, rows * h : rows * h + rows] * SCALE + bias
        e = jnp.exp2(s - jnp.max(s, axis=-1, keepdims=True))
        powers.append(e.astype(BF))
        scale.append(1.0 / jnp.sum(e, axis=-1, keepdims=True))
    empty = jnp.zeros((rows, 4 * HD), BF)
    values = jnp.concatenate(
        [jnp.where((lane >= HD * h) & (lane < HD * h + HD), v, empty) for h in range(GROUP)], axis=0
    )
    out = jnp.dot(jnp.concatenate(powers, axis=1), values, preferred_element_type=F32)
    left = out[:, : 2 * HD] * jnp.where(low, scale[0], scale[1])
    right = out[:, 2 * HD :] * jnp.where(low, scale[2], scale[3])
    return jnp.concatenate([left.astype(BF), right.astype(BF)], axis=1)


def kernel(
    counts, feats, wq_hbm, wo_hbm, gain, lscale, blend, out,
    wq, wo_own, wo_oth, x, nin, crop, qkv, heads, heads_in, heads2,
    upd_out, upd_in, fin_out, fin_in, bias,
    s_feat, s_wq, s_wo, s_out, h_send, h_recv, c_send, c_recv, u_send, u_recv, f_send, f_recv,
    x_send, x_recv, n_send, n_recv, b_send, b_recv,
):
    gy, gx, tp = lax.axis_index("gy"), lax.axis_index("gx"), lax.axis_index("tp")
    core, z, x_hi = gy % 2, (gy // 2) % 4, gy // 8
    dim = feats.shape[-1]
    tok = 256
    half = wo_hbm.shape[1]
    ng = half // 256

    def at_z(step):
        return (x_hi * 8 + ((z + step) % 4) * 2 + core, gx, tp)

    def at_y(step):
        return (gy, (gx + step) % 4, tp)

    twin = (gy + 1 - 2 * core, gx, tp)
    mate = (gy, gx, 1 - tp)
    mate_b = ((gy + 8) % 16, gx, 1 - tp)

    def remote(src, dst, ss, rs, dev):
        return pltpu.make_async_remote_copy(
            src_ref=src, dst_ref=dst, send_sem=ss, recv_sem=rs, device_id=dev, device_id_type=MESH
        )

    images = [3 * (1 - tp), 3 * tp, 1, 2]

    def quad(ref, image, t):
        return ref.at[image, pl.ds(8 * (t % 2), 8), pl.ds(8 * (t // 2), 8), :]

    def feat_copy(slot, t):
        return pltpu.make_async_copy(quad(feats, images[slot], t), x.at[slot, t], s_feat.at[slot, t])

    def out_copy(slot, t):
        return pltpu.make_async_copy(x.at[slot, t], quad(out, images[slot], t), s_out.at[slot, t])

    def wq_copy(layer, g):
        i = ng * layer + g
        return pltpu.make_async_copy(wq_hbm.at[layer, :, :, pl.ds(256 * g, 256)], wq.at[i], s_wq.at[i])

    def wo_copy(layer):
        return pltpu.make_async_copy(wo_hbm.at[layer], wo_own.at[layer], s_wo.at[layer])

    for t in range(4):
        feat_copy(0, t).start()
    for g in range(ng):
        wq_copy(0, g).start()

    barrier = pltpu.get_barrier_semaphore()

    def greet(dev):
        pl.semaphore_signal(barrier, inc=1, device_id=dev, device_id_type=MESH)

    for dev in (mate, mate_b, twin, at_z(1), at_z(-1), at_y(1), at_y(-1)):
        greet(dev)

    @pl.when(gy > 0)
    def _():
        greet((gy - 1, gx, tp))
        greet((gy - 1, (gx + 3) % 4, tp))

    @pl.when(gy < 15)
    def _():
        greet((gy + 1, gx, tp))
        greet((gy + 1, (gx + 1) % 4, tp))

    @pl.when(gy == 8)
    def _():
        greet((gy - 1, gx, 1 - tp))
        greet((gy - 1, (gx + 3) % 4, 1 - tp))

    @pl.when(gy == 7)
    def _():
        greet((gy + 1, gx, 1 - tp))
        greet((gy + 1, (gx + 1) % 4, 1 - tp))

    def side(k, p, edge):
        if k == 0 or p == 2:
            return tp
        return jnp.where(gy == edge, 1 - tp, tp)

    token = lax.broadcasted_iota(jnp.int32, (8, tok), 1)
    t_of, rr, cc = token // 64, (token % 64) // 8, token % 8

    def place(t):
        return (8 * (t % 2) + rr) * 16 + 8 * (t // 2) + cc

    bias[0] = jnp.where(place(t_of) < counts[gx, gy], 0.0, -1e30)
    below, right = jnp.minimum(gy + 1, 15), jnp.minimum(gx + 1, 3)
    in_y, in_x = gy < 15, gx < 3
    limit = jnp.full((8, tok), counts[gx, gy], jnp.int32)
    limit = jnp.where(t_of == 1, jnp.where(in_y, counts[gx, below], 0), limit)
    limit = jnp.where(t_of == 2, jnp.where(in_x, counts[right, gy], 0), limit)
    limit = jnp.where(t_of == 3, jnp.where(in_y & in_x, counts[right, below], 0), limit)
    bias[1] = jnp.where(place(3 - t_of) < limit, 0.0, -1e30)

    for slot in range(1, 4):
        for t in range(4):
            feat_copy(slot, t).start()
    wo_copy(0).start()

    @pl.when(gy == 0)
    def _():
        for k in range(3):
            upd_in[k, 0] = jnp.zeros((64, dim), BF)
            upd_in[k, 2] = jnp.zeros((64, dim), BF)

    @pl.when(gy == 15)
    def _():
        for k in range(3):
            crop[k, 64:128] = jnp.zeros((64, dim), BF)
            crop[k, 192:256] = jnp.zeros((64, dim), BF)

    pl.semaphore_wait(barrier, 7 + jnp.where(gy > 0, 2, 0) + jnp.where(gy < 15, 2, 0) + jnp.where((gy == 7) | (gy == 8), 2, 0))

    def piece(s, col, part, rows_of):
        kind, idx = STAGES[s]
        depth = dim if kind == "q" else half
        per = depth // 8
        base = (col % 4) * (2 * per) + core * per
        size = per
        if part is not None:
            size = per // 2
            base = base + part * size
        rows = pl.ds(pl.multiple_of(base, 16), size)
        if kind == "q":
            if rows_of == "src":
                return wq_hbm.at[1, :, rows, pl.ds(256 * idx, 256)]
            return wq.at[2 * ng + idx, :, rows, :]
        if rows_of == "src":
            return wo_hbm.at[idx, rows, :]
        return wo_oth.at[idx, rows, :]

    def along_y(s):
        return s in (0, 2)

    def colour(s):
        return (gx + 2 * z) % 4 if along_y(s) else (z + 2 * gx) % 4

    def x_copies(s):
        col = colour(s)
        if s < 3:
            return [
                remote(piece(s, col, i, "src"), piece(s, col, i, "dst"), x_send.at[s, i], x_recv.at[s, i], dev)
                for i, dev in enumerate((mate, mate_b))
            ]
        return [remote(piece(s, col, None, "src"), piece(s, col, None, "dst"), x_send.at[s, 1], x_recv.at[s, 1], mate_b)]

    def n_copies(s, arriving=False):
        col = colour(s)
        near, far = (at_y, at_z) if along_y(s) else (at_z, at_y)
        plan = ((near(1), None, col - 1), (near(-1), None, col + 1), (far(1), 0, col + 2), (far(-1), 1, col + 2))
        res = []
        for i, (dev, part, other) in enumerate(plan):
            ref = piece(s, (other + 4) if arriving else col, part, "dst")
            res.append(remote(ref, ref, n_send.at[s, i], n_recv.at[s, i], dev))
        return res

    def b_copy(s, i):
        col = colour(s) + (0, 3, 1, 2)[i]
        ref = piece(s, col, None, "dst")
        return remote(ref, ref, b_send.at[s, i], b_recv.at[s, i], twin)

    def b_arrival(s, i):
        kind, idx = STAGES[s]
        depth = dim if kind == "q" else half
        per = depth // 8
        col = colour(s) + (0, 3, 1, 2)[i]
        rows = pl.ds(pl.multiple_of((col % 4) * (2 * per) + (1 - core) * per, 16), per)
        ref = wq.at[2 * ng + idx, :, rows, :] if kind == "q" else wo_oth.at[idx, rows, :]
        return remote(ref, ref, b_send.at[s, i], b_recv.at[s, i], twin)

    def first_hop(s):
        for c in x_copies(s):
            c.start()

    def second_hop(s):
        for c in x_copies(s):
            c.wait_recv()
        for c in n_copies(s):
            c.start()
        b_copy(s, 0).start()

    def third_hop(s):
        for c in n_copies(s, arriving=True):
            c.wait_recv()
        for i in (1, 2, 3):
            b_copy(s, i).start()

    def arrived(s):
        for i in range(4):
            b_arrival(s, i).wait_recv()

    first_hop(0)
    first_hop(1)
    first_hop(2)
    for g in range(ng):
        wq_copy(1, g).start()
    wo_copy(1).start()

    def norm_into(slot, layer):
        for t in range(4):
            nin[slot, 64 * t : 64 * t + 64] = layer_norm(x[slot, t].reshape(64, dim), gain[layer : layer + 1, :])

    def project_in(n, w):
        return [jnp.dot(n, wq[w, j], preferred_element_type=F32).astype(BF) for j in range(3)]

    def keep(parts):
        for j in range(3):
            qkv[j] = parts[j]

    def heads_copy(idx, g):
        job = jnp.where(idx == 0, 0, idx + 1)
        return remote(heads.at[job, g], heads_in.at[idx, g], h_send.at[idx, g], h_recv.at[idx, g], mate)

    def feats_ready(slot):
        for t in range(4):
            feat_copy(slot, t).wait()

    feats_ready(0)
    norm_into(0, 0)
    wq_copy(0, 0).wait()
    keep(project_in(nin[0], 0))

    steps = 4 * ng

    def first_step(i, carry):
        job, g = i // ng, i % ng

        for slot in range(1, 4):

            @pl.when(i == ng * (slot - 1))
            def _(slot=slot):
                feats_ready(slot)
                norm_into(slot, 0)

        for w in range(1, ng):

            @pl.when(i == w - 1)
            def _(w=w):
                wq_copy(0, w).wait()

        later = jnp.minimum(i + 1, steps - 1)
        parts = project_in(nin[later // ng], later % ng)
        heads[job, g] = attend(qkv[0], qkv[1], qkv[2], bias[0, 0:1, :])
        keep(parts)

        @pl.when(job != 1)
        def _():
            heads_copy(jnp.where(job == 0, 0, job - 1), g).start()

        @pl.when(i == 2)
        def _():
            second_hop(0)

        @pl.when(i == 5)
        def _():
            second_hop(1)
            first_hop(3)

        @pl.when(i == 7)
        def _():
            third_hop(0)

        @pl.when(i == 8)
        def _():
            second_hop(2)

        @pl.when(i == 10)
        def _():
            third_hop(1)
            first_hop(4)

        return carry

    def crop_copy(k, p):
        dev = (gy - (p % 2), (gx + 4 - p // 2) % 4, side(k, p, 8))
        return remote(
            nin.at[k + 1, pl.ds(64 * (3 - p), 64), :], crop.at[k, pl.ds(64 * p, 64), :],
            c_send.at[k, p - 1], c_recv.at[k, p - 1], dev,
        )

    def finish_first(k):
        for g in range(ng):
            heads_copy(k, g).wait_recv()
        own = jnp.concatenate([heads[k + 1, g] for g in range(ng)], axis=1)
        oth = jnp.concatenate([heads_in[k, g] for g in range(ng)], axis=1)

        def chunk(c, carry):
            cols = pl.ds(pl.multiple_of(c * 512, 512), 512)
            acc = jnp.dot(own, wo_own[0, :, cols], preferred_element_type=F32)
            acc = acc + jnp.dot(oth, wo_oth[0, :, cols], preferred_element_type=F32)
            acc = acc * lscale[0:1, cols]
            x[k + 1, :, :, :, cols] += acc.reshape(4, 8, 8, 512)
            if k == 0:
                fin_out[:, cols] = acc.astype(BF)
            return carry

        lax.fori_loop(0, dim // 512, chunk, 0)
        norm_into(k + 1, 1)
        crop_copy(k, 2).start()

        @pl.when(gy > 0)
        def _():
            crop_copy(k, 3).start()
            crop_copy(k, 1).start()

        crop[k, 0:64] = nin[k + 1, 192:256]

    lax.fori_loop(0, steps, first_step, 0)
    wo_copy(0).wait()
    arrived(0)
    finish_first(0)
    second_hop(3)
    third_hop(2)
    for g in range(ng):
        wq_copy(1, g).wait()
    wo_copy(1).wait()
    second_hop(4)
    finish_first(1)
    third_hop(3)

    def upd_copy(k, p):
        dev = (gy + (p % 2), (gx + p // 2) % 4, side(k, p, 7))
        return remote(upd_out.at[k, p - 1], upd_in.at[k, 3 - p], u_send.at[k, p - 1], u_recv.at[k, p - 1], dev)

    def fin_copy(t):
        return remote(fin_out.at[pl.ds(64 * t, 64), :], fin_in.at[t], f_send.at[t], f_recv.at[t], mate)

    def crop_ready(k):
        crop_copy(k, 2).wait_recv()

        @pl.when(gy < 15)
        def _():
            crop_copy(k, 1).wait_recv()
            crop_copy(k, 3).wait_recv()

    def attend_crop(k):
        crop_ready(k)
        keep(project_in(crop[k], ng))

        def step(g, carry):
            if k == 0:

                @pl.when(g == 2)
                def _():
                    arrived(1)

                @pl.when(g == 3)
                def _():
                    finish_first(2)
                    third_hop(4)
                    arrived(2)

                @pl.when(g == 4)
                def _():
                    arrived(3)

            parts = project_in(crop[k], ng + g + 1)
            heads2[g] = attend(qkv[0], qkv[1], qkv[2], bias[1, 0:1, :])
            keep(parts)
            return carry

        lax.fori_loop(0, 2 * ng - 1, step, 0)
        heads2[2 * ng - 1] = attend(qkv[0], qkv[1], qkv[2], bias[1, 0:1, :])

    def project_crop(k):
        for lo in (128, 0):
            own = jnp.concatenate([heads2[g, lo : lo + 128] for g in range(ng)], axis=1)
            oth = jnp.concatenate([heads2[ng + g, lo : lo + 128] for g in range(ng)], axis=1)

            def chunk(c, carry, lo=lo, own=own, oth=oth):
                cols = pl.ds(pl.multiple_of(c * 512, 512), 512)
                acc = jnp.dot(own, wo_own[1, :, cols], preferred_element_type=F32)
                acc = acc + jnp.dot(oth, wo_oth[1, :, cols], preferred_element_type=F32)
                weight = jnp.concatenate([blend[lo : lo + 128]] * 4, axis=1)
                acc = acc * (lscale[1:2, cols] * weight)
                if lo == 0:
                    x[k + 1, 3, :, :, cols] += acc[:64].reshape(8, 8, 512)
                    upd_out[k, 0, :, cols] = acc[64:].astype(BF)
                    if k == 0:
                        fin_out[192:256, cols] = (fin_out[192:256, cols].astype(F32) + acc[:64]).astype(BF)
                else:
                    upd_out[k, 1, :, cols] = acc[:64].astype(BF)
                    upd_out[k, 2, :, cols] = acc[64:].astype(BF)
                return carry

            lax.fori_loop(0, dim // 512, chunk, 0)
            if lo == 128:
                upd_copy(k, 2).start()

                @pl.when(gy < 15)
                def _():
                    upd_copy(k, 3).start()
            else:

                @pl.when(gy < 15)
                def _():
                    upd_copy(k, 1).start()

                out_copy(k + 1, 3).start()
                if k == 0:
                    fin_copy(3).start()

    def blend_in(k):
        upd_copy(k, 2).wait_recv()

        @pl.when(gy > 0)
        def _():
            upd_copy(k, 1).wait_recv()
            upd_copy(k, 3).wait_recv()

        for t in (0, 1, 2):
            come = upd_in[k, t].astype(F32)
            if t < 2:
                come = jnp.where(gx > 0, come, 0.0)
            x[k + 1, t] += come.reshape(8, 8, dim)
            if k == 0:
                rows = slice(64 * t, 64 * t + 64)
                fin_out[rows] = (fin_out[rows].astype(F32) + come).astype(BF)
                fin_copy(t).start()
            out_copy(k + 1, t).start()

    attend_crop(0)
    arrived(4)
    project_crop(0)
    attend_crop(1)
    project_crop(1)
    blend_in(0)
    attend_crop(2)
    project_crop(2)
    blend_in(1)
    for t in (3, 0, 1, 2):
        fin_copy(t).wait_recv()
        x[0, t] += fin_in[t].astype(F32).reshape(8, 8, dim)
        out_copy(0, t).start()
    blend_in(2)

    for s in range(len(STAGES)):
        for c in x_copies(s):
            c.wait_send()
        for c in n_copies(s):
            c.wait_send()
        for i in range(4):
            b_copy(s, i).wait_send()
    for k in range(3):
        for g in range(ng):
            heads_copy(k, g).wait_send()
        crop_copy(k, 2).wait_send()
        upd_copy(k, 2).wait_send()

        @pl.when(gy > 0)
        def _():
            crop_copy(k, 1).wait_send()
            crop_copy(k, 3).wait_send()

        @pl.when(gy < 15)
        def _():
            upd_copy(k, 1).wait_send()
            upd_copy(k, 3).wait_send()

    for t in range(4):
        fin_copy(t).wait_send()
        for slot in range(4):
            out_copy(slot, t).wait()


def blend_rows():
    token = np.arange(256)
    t, rr, cc = token // 64, (token % 64) // 8, token % 8
    r, c = 8 * (t % 2) + rr, 8 * (t // 2) + cc
    row = np.sin(np.pi * (r.astype(np.float32) + 0.5) / 16) ** 2
    col = np.sin(np.pi * (c.astype(np.float32) + 0.5) / 16) ** 2
    weight = (0.25 + 0.75 * row * col).astype(np.float32)
    return np.broadcast_to(weight[:, None], (256, 128)).copy()


def copy_kernel(src, dst, sems):
    parts = [pltpu.make_async_copy(src.at[i], dst.at[i], sems.at[i]) for i in range(4)]
    for c in parts:
        c.start()
    for c in parts:
        c.wait()


def shards(features, qkv_weight, out_weight, norm_gain, layer_scale, valid_counts):
    dim = features.shape[-1]
    half = out_weight.shape[1]
    ng = half // 256
    anywhere = pl.BlockSpec(memory_space=pl.ANY)
    vmem = pl.BlockSpec(memory_space=pltpu.VMEM)
    dma = pltpu.SemaphoreType.DMA
    ns = len(STAGES)
    result = pl.pallas_call(
        kernel,
        out_shape=jax.ShapeDtypeStruct(features.shape, F32),
        in_specs=[pl.BlockSpec(memory_space=pltpu.SMEM), anywhere, anywhere, anywhere, vmem, vmem, vmem],
        out_specs=anywhere,
        scratch_shapes=[
            pltpu.VMEM((3 * ng, 3, dim, 256), BF),
            pltpu.VMEM((2, half, dim), BF),
            pltpu.VMEM((2, half, dim), BF),
            pltpu.VMEM((4, 4, 8, 8, dim), F32),
            pltpu.VMEM((4, 256, dim), BF),
            pltpu.VMEM((3, 256, dim), BF),
            pltpu.VMEM((3, 256, 256), BF),
            pltpu.VMEM((4, ng, 256, 256), BF),
            pltpu.VMEM((3, ng, 256, 256), BF),
            pltpu.VMEM((2 * ng, 256, 256), BF),
            pltpu.VMEM((3, 3, 64, dim), BF),
            pltpu.VMEM((3, 3, 64, dim), BF),
            pltpu.VMEM((256, dim), BF),
            pltpu.VMEM((4, 64, dim), BF),
            pltpu.VMEM((2, 8, 256), F32),
            dma((4, 4)), dma((2 * ng,)), dma((2,)), dma((4, 4)),
            dma((3, ng)), dma((3, ng)), dma((3, 3)), dma((3, 3)), dma((3, 3)), dma((3, 3)), dma((4,)), dma((4,)),
            dma((ns, 2)), dma((ns, 2)), dma((ns, 4)), dma((ns, 4)), dma((ns, 4)), dma((ns, 4)),
        ],
        compiler_params=pltpu.CompilerParams(
            collective_id=0, has_side_effects=True, vmem_limit_bytes=60 * 2**20
        ),
        name="two_sublayers",
    )(
        valid_counts.T, features, jnp.transpose(qkv_weight, (0, 2, 1, 3)), out_weight,
        norm_gain, layer_scale, jnp.asarray(blend_rows()),
    )
    return pl.pallas_call(
        copy_kernel,
        out_shape=jax.ShapeDtypeStruct(features.shape, F32),
        in_specs=[vmem],
        out_specs=anywhere,
        scratch_shapes=[dma((4,))],
        compiler_params=pltpu.CompilerParams(vmem_limit_bytes=16 * 2**20),
        name="result",
    )(result)


def solution(mesh):
    in_specs = (
        P(None, "gy", "gx", None),
        P(None, None, None, "tp"),
        P(None, "tp", None),
        P(),
        P(),
        P(),
    )
    out_specs = P(None, "gy", "gx", None)
    return jax.shard_map(shards, mesh=mesh, in_specs=in_specs, out_specs=out_specs, check_vma=False)
```

```python
import functools

import jax
import jax.numpy as jnp
import numpy as np
from jax import lax
from jax.experimental import pallas as pl
from jax.experimental.pallas import tpu as pltpu
from jax.sharding import PartitionSpec as P

F32 = jnp.float32
BF = jnp.bfloat16
MESH = pl.DeviceIdType.MESH
HD = 64
GROUP = 4
SCALE = HD**-0.5 * 1.4426950408889634
STAGES = (("o", 0), ("q", 0), ("q", 1), ("q", 2), ("o", 1))


def layer_norm(v, gain):
    centred = v - jnp.mean(v, axis=-1, keepdims=True)
    spread = jnp.mean(centred * centred, axis=-1, keepdims=True)
    return (centred * lax.rsqrt(spread + 1e-06) * gain).astype(BF)


def attend(q, k, v, bias):
    rows = q.shape[0]
    lane = lax.broadcasted_iota(jnp.int32, (rows, 4 * HD), 1)
    low = lax.broadcasted_iota(jnp.int32, (rows, 2 * HD), 1) < HD
    keys = k.T
    none = jnp.zeros((HD, rows), BF)
    keys = jnp.concatenate(
        [
            jnp.concatenate([keys[HD * h : HD * h + HD] if g == h else none for g in range(GROUP)], axis=0)
            for h in range(GROUP)
        ],
        axis=1,
    )
    scores = jnp.dot(q, keys, preferred_element_type=F32)
    powers, scale = [], []
    for h in range(GROUP):
        s = scores[:, rows * h : rows * h + rows] * SCALE + bias
        e = jnp.exp2(s - jnp.max(s, axis=-1, keepdims=True))
        powers.append(e.astype(BF))
        scale.append(1.0 / jnp.sum(e, axis=-1, keepdims=True))
    empty = jnp.zeros((rows, 4 * HD), BF)
    values = jnp.concatenate(
        [jnp.where((lane >= HD * h) & (lane < HD * h + HD), v, empty) for h in range(GROUP)], axis=0
    )
    out = jnp.dot(jnp.concatenate(powers, axis=1), values, preferred_element_type=F32)
    left = out[:, : 2 * HD] * jnp.where(low, scale[0], scale[1])
    right = out[:, 2 * HD :] * jnp.where(low, scale[2], scale[3])
    return jnp.concatenate([left.astype(BF), right.astype(BF)], axis=1)


def images_of(gy, tp):
    pick = jnp.where(gy < 8, tp, 1 - tp)
    return [3 * (1 - pick), 3 * pick, 1, 2]


def quad(ref, image, t):
    return ref.at[image, pl.ds(8 * (t % 2), 8), pl.ds(8 * (t // 2), 8), :]


def kernel(
    counts, feats, wq_hbm, wo_hbm, gain, lscale, blend, x,
    wq, wo_own, wo_oth, nin, crop, qkv, heads, heads_in, heads2,
    upd_out, upd_in, fin_out, fin_in, bias,
    s_feat, s_wq, s_wo, h_send, h_recv, c_send, c_recv, u_send, u_recv, f_send, f_recv,
    x_send, x_recv, n_send, n_recv, b_send, b_recv,
):
    gy, gx, tp = lax.axis_index("gy"), lax.axis_index("gx"), lax.axis_index("tp")
    core, z, x_hi = gy % 2, (gy // 2) % 4, gy // 8
    dim = feats.shape[-1]
    tok = 256
    half = wo_hbm.shape[1]
    ng = half // 256

    def at_z(step):
        return (x_hi * 8 + ((z + step) % 4) * 2 + core, gx, tp)

    def at_y(step):
        return (gy, (gx + step) % 4, tp)

    twin = (gy + 1 - 2 * core, gx, tp)
    mate = (gy, gx, 1 - tp)
    mate_b = ((gy + 8) % 16, gx, 1 - tp)

    def remote(src, dst, ss, rs, dev):
        return pltpu.make_async_remote_copy(
            src_ref=src, dst_ref=dst, send_sem=ss, recv_sem=rs, device_id=dev, device_id_type=MESH
        )

    images = images_of(gy, tp)

    def feat_copy(slot, t):
        return pltpu.make_async_copy(quad(feats, images[slot], t), x.at[slot, t], s_feat.at[slot, t])

    def wq_copy(layer, g):
        i = ng * layer + g
        return pltpu.make_async_copy(wq_hbm.at[layer, :, :, pl.ds(256 * g, 256)], wq.at[i], s_wq.at[i])

    def wo_copy(layer):
        return pltpu.make_async_copy(wo_hbm.at[layer], wo_own.at[layer], s_wo.at[layer])

    for t in range(4):
        feat_copy(0, t).start()
    for g in range(ng):
        wq_copy(0, g).start()

    barrier = pltpu.get_barrier_semaphore()

    def greet(dev):
        pl.semaphore_signal(barrier, inc=1, device_id=dev, device_id_type=MESH)

    for dev in (mate, mate_b, twin, at_z(1), at_z(-1), at_y(1), at_y(-1)):
        greet(dev)

    @pl.when(gy > 0)
    def _():
        greet((gy - 1, gx, tp))
        greet((gy - 1, (gx + 3) % 4, tp))

    @pl.when(gy < 15)
    def _():
        greet((gy + 1, gx, tp))
        greet((gy + 1, (gx + 1) % 4, tp))

    @pl.when(gy == 8)
    def _():
        greet((gy - 1, gx, 1 - tp))
        greet((gy - 1, (gx + 3) % 4, 1 - tp))

    @pl.when(gy == 7)
    def _():
        greet((gy + 1, gx, 1 - tp))
        greet((gy + 1, (gx + 1) % 4, 1 - tp))

    def side(p, edge):
        if p == 2:
            return tp
        return jnp.where(gy == edge, 1 - tp, tp)

    token = lax.broadcasted_iota(jnp.int32, (8, tok), 1)
    t_of, rr, cc = token // 64, (token % 64) // 8, token % 8

    def place(t):
        return (8 * (t % 2) + rr) * 16 + 8 * (t // 2) + cc

    bias[0] = jnp.where(place(t_of) < counts[gx, gy], 0.0, -1e30)
    below, right = jnp.minimum(gy + 1, 15), jnp.minimum(gx + 1, 3)
    in_y, in_x = gy < 15, gx < 3
    limit = jnp.full((8, tok), counts[gx, gy], jnp.int32)
    limit = jnp.where(t_of == 1, jnp.where(in_y, counts[gx, below], 0), limit)
    limit = jnp.where(t_of == 2, jnp.where(in_x, counts[right, gy], 0), limit)
    limit = jnp.where(t_of == 3, jnp.where(in_y & in_x, counts[right, below], 0), limit)
    bias[1] = jnp.where(place(3 - t_of) < limit, 0.0, -1e30)

    for slot in range(1, 4):
        for t in range(4):
            feat_copy(slot, t).start()
    wo_copy(0).start()

    @pl.when(gy == 0)
    def _():
        for k in range(3):
            upd_in[k, 0] = jnp.zeros((64, dim), BF)
            upd_in[k, 2] = jnp.zeros((64, dim), BF)

    @pl.when(gy == 15)
    def _():
        for k in range(3):
            crop[k, 64:128] = jnp.zeros((64, dim), BF)
            crop[k, 192:256] = jnp.zeros((64, dim), BF)

    pl.semaphore_wait(barrier, 7 + jnp.where(gy > 0, 2, 0) + jnp.where(gy < 15, 2, 0) + jnp.where((gy == 7) | (gy == 8), 2, 0))

    def piece(s, col, part, rows_of):
        kind, idx = STAGES[s]
        depth = dim if kind == "q" else half
        per = depth // 8
        base = (col % 4) * (2 * per) + core * per
        size = per
        if part is not None:
            size = per // 2
            base = base + part * size
        rows = pl.ds(pl.multiple_of(base, 16), size)
        if kind == "q":
            if rows_of == "src":
                return wq_hbm.at[1, :, rows, pl.ds(256 * idx, 256)]
            return wq.at[2 * ng + idx, :, rows, :]
        if rows_of == "src":
            return wo_hbm.at[idx, rows, :]
        return wo_oth.at[idx, rows, :]

    def along_y(s):
        return s in (0, 2)

    def colour(s):
        return (gx + 2 * z) % 4 if along_y(s) else (z + 2 * gx) % 4

    def x_copies(s):
        col = colour(s)
        if s < 3:
            return [
                remote(piece(s, col, i, "src"), piece(s, col, i, "dst"), x_send.at[s, i], x_recv.at[s, i], dev)
                for i, dev in enumerate((mate, mate_b))
            ]
        return [remote(piece(s, col, None, "src"), piece(s, col, None, "dst"), x_send.at[s, 1], x_recv.at[s, 1], mate_b)]

    def n_copies(s, arriving=False):
        col = colour(s)
        near, far = (at_y, at_z) if along_y(s) else (at_z, at_y)
        plan = ((near(1), None, col - 1), (near(-1), None, col + 1), (far(1), 0, col + 2), (far(-1), 1, col + 2))
        res = []
        for i, (dev, part, other) in enumerate(plan):
            ref = piece(s, (other + 4) if arriving else col, part, "dst")
            res.append(remote(ref, ref, n_send.at[s, i], n_recv.at[s, i], dev))
        return res

    def b_copy(s, i):
        col = colour(s) + (0, 3, 1, 2)[i]
        ref = piece(s, col, None, "dst")
        return remote(ref, ref, b_send.at[s, i], b_recv.at[s, i], twin)

    def b_arrival(s, i):
        kind, idx = STAGES[s]
        depth = dim if kind == "q" else half
        per = depth // 8
        col = colour(s) + (0, 3, 1, 2)[i]
        rows = pl.ds(pl.multiple_of((col % 4) * (2 * per) + (1 - core) * per, 16), per)
        ref = wq.at[2 * ng + idx, :, rows, :] if kind == "q" else wo_oth.at[idx, rows, :]
        return remote(ref, ref, b_send.at[s, i], b_recv.at[s, i], twin)

    def first_hop(s):
        for c in x_copies(s):
            c.start()

    def second_hop(s):
        for c in x_copies(s):
            c.wait_recv()
        for c in n_copies(s):
            c.start()
        b_copy(s, 0).start()

    def third_hop(s):
        for c in n_copies(s, arriving=True):
            c.wait_recv()
        for i in (1, 2, 3):
            b_copy(s, i).start()

    def arrived(s):
        for i in range(4):
            b_arrival(s, i).wait_recv()

    first_hop(0)
    first_hop(1)
    first_hop(2)
    for g in range(ng):
        wq_copy(1, g).start()
    wo_copy(1).start()

    def norm_into(slot, layer, quarters=range(4)):
        for t in quarters:
            nin[slot, 64 * t : 64 * t + 64] = layer_norm(x[slot, t].reshape(64, dim), gain[layer : layer + 1, :])

    def project_in(n, w):
        return [jnp.dot(n, wq[w, j], preferred_element_type=F32).astype(BF) for j in range(3)]

    def keep(parts):
        for j in range(3):
            qkv[j] = parts[j]

    def heads_copy(idx, g):
        job = jnp.where(idx == 0, 0, idx + 1)
        return remote(heads.at[job, g], heads_in.at[idx, g], h_send.at[idx, g], h_recv.at[idx, g], mate)

    def feats_ready(slot):
        for t in range(4):
            feat_copy(slot, t).wait()

    feats_ready(0)
    norm_into(0, 0)
    wq_copy(0, 0).wait()
    keep(project_in(nin[0], 0))

    steps = 4 * ng

    def first_step(i, carry):
        job, g = i // ng, i % ng

        for slot in range(1, 4):

            @pl.when(i == ng * (slot - 1))
            def _(slot=slot):
                feats_ready(slot)
                norm_into(slot, 0)

        for w in range(1, ng):

            @pl.when(i == w - 1)
            def _(w=w):
                wq_copy(0, w).wait()

        later = jnp.minimum(i + 1, steps - 1)
        parts = project_in(nin[later // ng], later % ng)
        heads[job, g] = attend(qkv[0], qkv[1], qkv[2], bias[0, 0:1, :])
        keep(parts)

        @pl.when(job != 1)
        def _():
            heads_copy(jnp.where(job == 0, 0, job - 1), g).start()

        @pl.when(i == 2)
        def _():
            second_hop(0)

        @pl.when(i == 5)
        def _():
            second_hop(1)
            first_hop(3)

        @pl.when(i == 7)
        def _():
            third_hop(0)

        @pl.when(i == 8)
        def _():
            second_hop(2)

        @pl.when(i == 10)
        def _():
            third_hop(1)
            first_hop(4)

        return carry

    def crop_copy(k, p):
        dev = (gy - (p % 2), (gx + 4 - p // 2) % 4, side(p, 8))
        return remote(
            nin.at[k + 1, pl.ds(64 * (3 - p), 64), :], crop.at[k, pl.ds(64 * p, 64), :],
            c_send.at[k, p - 1], c_recv.at[k, p - 1], dev,
        )

    def finish_first(k):
        for g in range(ng):
            heads_copy(k, g).wait_recv()
        for lo in (0, 2):
            rows = slice(64 * lo, 64 * lo + 128)
            own = jnp.concatenate([heads[k + 1, g, rows] for g in range(ng)], axis=1)
            oth = jnp.concatenate([heads_in[k, g, rows] for g in range(ng)], axis=1)

            def chunk(c, carry, lo=lo, rows=rows, own=own, oth=oth):
                cols = pl.ds(pl.multiple_of(c * 512, 512), 512)
                acc = jnp.dot(own, wo_own[0, :, cols], preferred_element_type=F32)
                acc = acc + jnp.dot(oth, wo_oth[0, :, cols], preferred_element_type=F32)
                acc = acc * lscale[0:1, cols]
                x[k + 1, lo : lo + 2, :, :, cols] += acc.reshape(2, 8, 8, 512)
                if k == 0:
                    fin_out[rows, cols] = acc.astype(BF)
                return carry

            lax.fori_loop(0, dim // 512, chunk, 0)
            norm_into(k + 1, 1, (lo, lo + 1))
            if lo == 0:
                crop_copy(k, 2).start()

                @pl.when(gy > 0)
                def _():
                    crop_copy(k, 3).start()
            else:

                @pl.when(gy > 0)
                def _():
                    crop_copy(k, 1).start()

        crop[k, 0:64] = nin[k + 1, 192:256]

    lax.fori_loop(0, steps, first_step, 0)
    wo_copy(0).wait()
    arrived(0)
    finish_first(0)
    second_hop(3)
    third_hop(2)
    for g in range(ng):
        wq_copy(1, g).wait()
    wo_copy(1).wait()
    second_hop(4)
    finish_first(1)
    third_hop(3)

    def upd_copy(k, p):
        dev = (gy + (p % 2), (gx + p // 2) % 4, side(p, 7))
        return remote(upd_out.at[k, p - 1], upd_in.at[k, 3 - p], u_send.at[k, p - 1], u_recv.at[k, p - 1], dev)

    def fin_copy(t):
        return remote(fin_out.at[pl.ds(64 * t, 64), :], fin_in.at[t], f_send.at[t], f_recv.at[t], mate)

    def crop_ready(k):
        crop_copy(k, 2).wait_recv()

        @pl.when(gy < 15)
        def _():
            crop_copy(k, 1).wait_recv()
            crop_copy(k, 3).wait_recv()

    def attend_crop(k):
        crop_ready(k)
        keep(project_in(crop[k], ng))

        def step(g, carry):
            if k == 0:

                @pl.when(g == 2)
                def _():
                    arrived(1)

                @pl.when(g == 3)
                def _():
                    finish_first(2)
                    third_hop(4)
                    arrived(2)

                @pl.when(g == 4)
                def _():
                    arrived(3)

            parts = project_in(crop[k], ng + g + 1)
            heads2[g] = attend(qkv[0], qkv[1], qkv[2], bias[1, 0:1, :])
            keep(parts)
            return carry

        lax.fori_loop(0, 2 * ng - 1, step, 0)
        heads2[2 * ng - 1] = attend(qkv[0], qkv[1], qkv[2], bias[1, 0:1, :])

    def project_crop(k):
        for lo in (128, 0):
            own = jnp.concatenate([heads2[g, lo : lo + 128] for g in range(ng)], axis=1)
            oth = jnp.concatenate([heads2[ng + g, lo : lo + 128] for g in range(ng)], axis=1)

            def chunk(c, carry, lo=lo, own=own, oth=oth):
                cols = pl.ds(pl.multiple_of(c * 512, 512), 512)
                acc = jnp.dot(own, wo_own[1, :, cols], preferred_element_type=F32)
                acc = acc + jnp.dot(oth, wo_oth[1, :, cols], preferred_element_type=F32)
                weight = jnp.concatenate([blend[lo : lo + 128]] * 4, axis=1)
                acc = acc * (lscale[1:2, cols] * weight)
                if lo == 0:
                    x[k + 1, 3, :, :, cols] += acc[:64].reshape(8, 8, 512)
                    upd_out[k, 0, :, cols] = acc[64:].astype(BF)
                    if k == 0:
                        fin_out[192:256, cols] = (fin_out[192:256, cols].astype(F32) + acc[:64]).astype(BF)
                else:
                    upd_out[k, 1, :, cols] = acc[:64].astype(BF)
                    upd_out[k, 2, :, cols] = acc[64:].astype(BF)
                return carry

            lax.fori_loop(0, dim // 512, chunk, 0)
            if lo == 128:
                upd_copy(k, 2).start()

                @pl.when(gy < 15)
                def _():
                    upd_copy(k, 3).start()
            else:

                @pl.when(gy < 15)
                def _():
                    upd_copy(k, 1).start()

                if k == 0:
                    fin_copy(3).start()

    def blend_in(k):
        upd_copy(k, 2).wait_recv()

        @pl.when(gy > 0)
        def _():
            upd_copy(k, 1).wait_recv()
            upd_copy(k, 3).wait_recv()

        for t in (0, 1, 2):
            come = upd_in[k, t].astype(F32)
            if t < 2:
                come = jnp.where(gx > 0, come, 0.0)
            x[k + 1, t] += come.reshape(8, 8, dim)
            if k == 0:
                rows = slice(64 * t, 64 * t + 64)
                fin_out[rows] = (fin_out[rows].astype(F32) + come).astype(BF)
                fin_copy(t).start()

    attend_crop(0)
    arrived(4)
    project_crop(0)
    attend_crop(1)
    project_crop(1)
    blend_in(0)
    attend_crop(2)
    project_crop(2)
    blend_in(1)
    for t in (3, 0, 1, 2):
        fin_copy(t).wait_recv()
        x[0, t] += fin_in[t].astype(F32).reshape(8, 8, dim)
    blend_in(2)

    for s in range(len(STAGES)):
        for c in x_copies(s):
            c.wait_send()
        for c in n_copies(s):
            c.wait_send()
        for i in range(4):
            b_copy(s, i).wait_send()
    for k in range(3):
        for g in range(ng):
            heads_copy(k, g).wait_send()
        crop_copy(k, 2).wait_send()
        upd_copy(k, 2).wait_send()

        @pl.when(gy > 0)
        def _():
            crop_copy(k, 1).wait_send()
            crop_copy(k, 3).wait_send()

        @pl.when(gy < 15)
        def _():
            upd_copy(k, 1).wait_send()
            upd_copy(k, 3).wait_send()

    for t in range(4):
        fin_copy(t).wait_send()


def blend_rows():
    token = np.arange(256)
    t, rr, cc = token // 64, (token % 64) // 8, token % 8
    r, c = 8 * (t % 2) + rr, 8 * (t // 2) + cc
    row = np.sin(np.pi * (r.astype(np.float32) + 0.5) / 16) ** 2
    col = np.sin(np.pi * (c.astype(np.float32) + 0.5) / 16) ** 2
    weight = (0.25 + 0.75 * row * col).astype(np.float32)
    return np.broadcast_to(weight[:, None], (256, 128)).copy()


def copy_kernel(src, dst, sems):
    images = images_of(lax.axis_index("gy"), lax.axis_index("tp"))
    parts = [
        pltpu.make_async_copy(src.at[slot, t], quad(dst, images[slot], t), sems.at[slot, t])
        for slot in range(4)
        for t in range(4)
    ]
    for c in parts:
        c.start()
    for c in parts:
        c.wait()


def shards(features, qkv_weight, out_weight, norm_gain, layer_scale, valid_counts):
    dim = features.shape[-1]
    half = out_weight.shape[1]
    ng = half // 256
    anywhere = pl.BlockSpec(memory_space=pl.ANY)
    vmem = pl.BlockSpec(memory_space=pltpu.VMEM)
    dma = pltpu.SemaphoreType.DMA
    ns = len(STAGES)
    result = pl.pallas_call(
        kernel,
        out_shape=pltpu.VMEM((4, 4, 8, 8, dim), F32),
        in_specs=[pl.BlockSpec(memory_space=pltpu.SMEM), anywhere, anywhere, anywhere, vmem, vmem, vmem],
        out_specs=vmem,
        scratch_shapes=[
            pltpu.VMEM((3 * ng, 3, dim, 256), BF),
            pltpu.VMEM((2, half, dim), BF),
            pltpu.VMEM((2, half, dim), BF),
            pltpu.VMEM((4, 256, dim), BF),
            pltpu.VMEM((3, 256, dim), BF),
            pltpu.VMEM((3, 256, 256), BF),
            pltpu.VMEM((4, ng, 256, 256), BF),
            pltpu.VMEM((3, ng, 256, 256), BF),
            pltpu.VMEM((2 * ng, 256, 256), BF),
            pltpu.VMEM((3, 3, 64, dim), BF),
            pltpu.VMEM((3, 3, 64, dim), BF),
            pltpu.VMEM((256, dim), BF),
            pltpu.VMEM((4, 64, dim), BF),
            pltpu.VMEM((2, 8, 256), F32),
            dma((4, 4)), dma((2 * ng,)), dma((2,)),
            dma((3, ng)), dma((3, ng)), dma((3, 3)), dma((3, 3)), dma((3, 3)), dma((3, 3)), dma((4,)), dma((4,)),
            dma((ns, 2)), dma((ns, 2)), dma((ns, 4)), dma((ns, 4)), dma((ns, 4)), dma((ns, 4)),
        ],
        compiler_params=pltpu.CompilerParams(
            collective_id=0, has_side_effects=True, vmem_limit_bytes=54 * 2**20
        ),
        name="two_sublayers",
    )(
        valid_counts.T, features, jnp.transpose(qkv_weight, (0, 2, 1, 3)), out_weight,
        norm_gain, layer_scale, jnp.asarray(blend_rows()),
    )
    return pl.pallas_call(
        copy_kernel,
        out_shape=jax.ShapeDtypeStruct(features.shape, F32),
        in_specs=[vmem],
        out_specs=anywhere,
        scratch_shapes=[dma((4, 4))],
        compiler_params=pltpu.CompilerParams(vmem_limit_bytes=16 * 2**20),
        name="result",
    )(result)


def solution(mesh):
    in_specs = (
        P(None, "gy", "gx", None),
        P(None, None, None, "tp"),
        P(None, "tp", None),
        P(),
        P(),
        P(),
    )
    out_specs = P(None, "gy", "gx", None)
    return jax.shard_map(shards, mesh=mesh, in_specs=in_specs, out_specs=out_specs, check_vma=False)
```

```python
import functools

import jax
import jax.numpy as jnp
import numpy as np
from jax import lax
from jax.experimental import pallas as pl
from jax.experimental.pallas import tpu as pltpu
from jax.sharding import PartitionSpec as P

F32 = jnp.float32
BF = jnp.bfloat16
MESH = pl.DeviceIdType.MESH
HD = 64
GROUP = 4
SCALE = HD**-0.5 * 1.4426950408889634
STAGES = (("o", 0), ("q", 0), ("q", 1), ("q", 2), ("o", 1))


def layer_norm(v, gain):
    centred = v - jnp.mean(v, axis=-1, keepdims=True)
    spread = jnp.mean(centred * centred, axis=-1, keepdims=True)
    return (centred * lax.rsqrt(spread + 1e-06) * gain).astype(BF)


def attend(q, k, v, bias):
    rows = q.shape[0]
    lane = lax.broadcasted_iota(jnp.int32, (rows, 4 * HD), 1)
    low = lax.broadcasted_iota(jnp.int32, (rows, 2 * HD), 1) < HD
    keys = k.T
    none = jnp.zeros((HD, rows), BF)
    keys = jnp.concatenate(
        [
            jnp.concatenate([keys[HD * h : HD * h + HD] if g == h else none for g in range(GROUP)], axis=0)
            for h in range(GROUP)
        ],
        axis=1,
    )
    scores = jnp.dot(q, keys, preferred_element_type=F32)
    powers, scale = [], []
    for h in range(GROUP):
        s = scores[:, rows * h : rows * h + rows] * SCALE + bias
        e = jnp.exp2(s - jnp.max(s, axis=-1, keepdims=True))
        powers.append(e.astype(BF))
        scale.append(1.0 / jnp.sum(e, axis=-1, keepdims=True))
    empty = jnp.zeros((rows, 4 * HD), BF)
    values = jnp.concatenate(
        [jnp.where((lane >= HD * h) & (lane < HD * h + HD), v, empty) for h in range(GROUP)], axis=0
    )
    out = jnp.dot(jnp.concatenate(powers, axis=1), values, preferred_element_type=F32)
    left = out[:, : 2 * HD] * jnp.where(low, scale[0], scale[1])
    right = out[:, 2 * HD :] * jnp.where(low, scale[2], scale[3])
    return jnp.concatenate([left.astype(BF), right.astype(BF)], axis=1)


def images_of(gy, tp):
    pick = jnp.where(gy < 8, tp, 1 - tp)
    return [3 * (1 - pick), 3 * pick, 1, 2]


def quad(ref, image, t):
    return ref.at[image, pl.ds(8 * (t % 2), 8), pl.ds(8 * (t // 2), 8), :]


def kernel(
    counts, feats, wq_hbm, wo_hbm, gain, lscale, blend, x,
    wq, wo_own, wo_oth, nin, crop, qkv, heads, heads_in, heads2,
    upd_out, upd_in, fin_out, fin_in, bias,
    s_feat, s_wq, s_wo, h_send, h_recv, c_send, c_recv, u_send, u_recv, f_send, f_recv,
    x_send, x_recv, n_send, n_recv, b_send, b_recv,
):
    gy, gx, tp = lax.axis_index("gy"), lax.axis_index("gx"), lax.axis_index("tp")
    core, z, x_hi = gy % 2, (gy // 2) % 4, gy // 8
    dim = feats.shape[-1]
    tok = 256
    half = wo_hbm.shape[1]
    ng = half // 256

    def at_z(step):
        return (x_hi * 8 + ((z + step) % 4) * 2 + core, gx, tp)

    def at_y(step):
        return (gy, (gx + step) % 4, tp)

    twin = (gy + 1 - 2 * core, gx, tp)
    mate = (gy, gx, 1 - tp)
    mate_b = ((gy + 8) % 16, gx, 1 - tp)

    def remote(src, dst, ss, rs, dev):
        return pltpu.make_async_remote_copy(
            src_ref=src, dst_ref=dst, send_sem=ss, recv_sem=rs, device_id=dev, device_id_type=MESH
        )

    images = images_of(gy, tp)

    def feat_copy(slot, t):
        return pltpu.make_async_copy(quad(feats, images[slot], t), x.at[slot, t], s_feat.at[slot, t])

    def wq_copy(layer, g):
        i = ng * layer + g
        return pltpu.make_async_copy(wq_hbm.at[layer, :, :, pl.ds(256 * g, 256)], wq.at[i], s_wq.at[i])

    def wo_copy(layer):
        return pltpu.make_async_copy(wo_hbm.at[layer], wo_own.at[layer], s_wo.at[layer])

    for t in range(4):
        feat_copy(0, t).start()
    for g in range(ng):
        wq_copy(0, g).start()

    barrier = pltpu.get_barrier_semaphore()

    def greet(dev):
        pl.semaphore_signal(barrier, inc=1, device_id=dev, device_id_type=MESH)

    for dev in (mate, mate_b, twin, at_z(1), at_z(-1), at_y(1), at_y(-1)):
        greet(dev)

    @pl.when(gy > 0)
    def _():
        greet((gy - 1, gx, tp))
        greet((gy - 1, (gx + 3) % 4, tp))

    @pl.when(gy < 15)
    def _():
        greet((gy + 1, gx, tp))
        greet((gy + 1, (gx + 1) % 4, tp))

    @pl.when(gy == 8)
    def _():
        greet((gy - 1, gx, 1 - tp))
        greet((gy - 1, (gx + 3) % 4, 1 - tp))

    @pl.when(gy == 7)
    def _():
        greet((gy + 1, gx, 1 - tp))
        greet((gy + 1, (gx + 1) % 4, 1 - tp))

    def side(p, edge):
        if p == 2:
            return tp
        return jnp.where(gy == edge, 1 - tp, tp)

    token = lax.broadcasted_iota(jnp.int32, (8, tok), 1)
    t_of, rr, cc = token // 64, (token % 64) // 8, token % 8

    def place(t):
        return (8 * (t % 2) + rr) * 16 + 8 * (t // 2) + cc

    bias[0] = jnp.where(place(t_of) < counts[gx, gy], 0.0, -1e30)
    below, right = jnp.minimum(gy + 1, 15), jnp.minimum(gx + 1, 3)
    in_y, in_x = gy < 15, gx < 3
    limit = jnp.full((8, tok), counts[gx, gy], jnp.int32)
    limit = jnp.where(t_of == 1, jnp.where(in_y, counts[gx, below], 0), limit)
    limit = jnp.where(t_of == 2, jnp.where(in_x, counts[right, gy], 0), limit)
    limit = jnp.where(t_of == 3, jnp.where(in_y & in_x, counts[right, below], 0), limit)
    bias[1] = jnp.where(place(3 - t_of) < limit, 0.0, -1e30)

    for slot in range(1, 4):
        for t in range(4):
            feat_copy(slot, t).start()
    wo_copy(0).start()

    @pl.when(gy == 0)
    def _():
        for k in range(3):
            upd_in[k, 0] = jnp.zeros((64, dim), BF)
            upd_in[k, 2] = jnp.zeros((64, dim), BF)

    @pl.when(gy == 15)
    def _():
        for k in range(3):
            crop[k, 64:128] = jnp.zeros((64, dim), BF)
            crop[k, 192:256] = jnp.zeros((64, dim), BF)

    pl.semaphore_wait(barrier, 7 + jnp.where(gy > 0, 2, 0) + jnp.where(gy < 15, 2, 0) + jnp.where((gy == 7) | (gy == 8), 2, 0))

    def piece(s, col, part, rows_of):
        kind, idx = STAGES[s]
        depth = dim if kind == "q" else half
        per = depth // 8
        base = (col % 4) * (2 * per) + core * per
        size = per
        if part is not None:
            size = per // 2
            base = base + part * size
        rows = pl.ds(pl.multiple_of(base, 16), size)
        if kind == "q":
            if rows_of == "src":
                return wq_hbm.at[1, :, rows, pl.ds(256 * idx, 256)]
            return wq.at[2 * ng + idx, :, rows, :]
        if rows_of == "src":
            return wo_hbm.at[idx, rows, :]
        return wo_oth.at[idx, rows, :]

    def along_y(s):
        return s in (0, 2)

    def colour(s):
        return (gx + 2 * z) % 4 if along_y(s) else (z + 2 * gx) % 4

    def x_copies(s):
        col = colour(s)
        if s < 3:
            return [
                remote(piece(s, col, i, "src"), piece(s, col, i, "dst"), x_send.at[s, i], x_recv.at[s, i], dev)
                for i, dev in enumerate((mate, mate_b))
            ]
        return [remote(piece(s, col, None, "src"), piece(s, col, None, "dst"), x_send.at[s, 1], x_recv.at[s, 1], mate_b)]

    def n_copies(s, arriving=False):
        col = colour(s)
        near, far = (at_y, at_z) if along_y(s) else (at_z, at_y)
        plan = ((near(1), None, col - 1), (near(-1), None, col + 1), (far(1), 0, col + 2), (far(-1), 1, col + 2))
        res = []
        for i, (dev, part, other) in enumerate(plan):
            ref = piece(s, (other + 4) if arriving else col, part, "dst")
            res.append(remote(ref, ref, n_send.at[s, i], n_recv.at[s, i], dev))
        return res

    def b_copy(s, i):
        col = colour(s) + (0, 3, 1, 2)[i]
        ref = piece(s, col, None, "dst")
        return remote(ref, ref, b_send.at[s, i], b_recv.at[s, i], twin)

    def b_arrival(s, i):
        kind, idx = STAGES[s]
        depth = dim if kind == "q" else half
        per = depth // 8
        col = colour(s) + (0, 3, 1, 2)[i]
        rows = pl.ds(pl.multiple_of((col % 4) * (2 * per) + (1 - core) * per, 16), per)
        ref = wq.at[2 * ng + idx, :, rows, :] if kind == "q" else wo_oth.at[idx, rows, :]
        return remote(ref, ref, b_send.at[s, i], b_recv.at[s, i], twin)

    def first_hop(s):
        for c in x_copies(s):
            c.start()

    def second_hop(s):
        for c in x_copies(s):
            c.wait_recv()
        for c in n_copies(s):
            c.start()
        b_copy(s, 0).start()

    def third_hop(s):
        for c in n_copies(s, arriving=True):
            c.wait_recv()
        for i in (1, 2, 3):
            b_copy(s, i).start()

    def arrived(s):
        for i in range(4):
            b_arrival(s, i).wait_recv()

    first_hop(0)
    first_hop(1)
    first_hop(2)

    def norm_into(slot, layer, quarters=range(4)):
        for t in quarters:
            nin[slot, 64 * t : 64 * t + 64] = layer_norm(x[slot, t].reshape(64, dim), gain[layer : layer + 1, :])

    def project_in(n, w):
        return [jnp.dot(n, wq[w, j], preferred_element_type=F32).astype(BF) for j in range(3)]

    def keep(parts):
        for j in range(3):
            qkv[j] = parts[j]

    def heads_copy(idx, g):
        job = jnp.where(idx == 0, 0, idx + 1)
        return remote(heads.at[job, g], heads_in.at[idx, g], h_send.at[idx, g], h_recv.at[idx, g], mate)

    def feats_ready(slot):
        for t in range(4):
            feat_copy(slot, t).wait()

    feats_ready(0)
    norm_into(0, 0)
    wq_copy(0, 0).wait()
    keep(project_in(nin[0], 0))

    steps = 4 * ng

    def first_step(i, carry):
        job, g = i // ng, i % ng

        for slot in range(1, 4):

            @pl.when(i == ng * (slot - 1))
            def _(slot=slot):
                feats_ready(slot)
                norm_into(slot, 0)

        for w in range(1, ng):

            @pl.when(i == w - 1)
            def _(w=w):
                wq_copy(0, w).wait()

        later = jnp.minimum(i + 1, steps - 1)
        parts = project_in(nin[later // ng], later % ng)
        heads[job, g] = attend(qkv[0], qkv[1], qkv[2], bias[0, 0:1, :])
        keep(parts)

        @pl.when(job != 1)
        def _():
            heads_copy(jnp.where(job == 0, 0, job - 1), g).start()

        @pl.when(i == 2)
        def _():
            second_hop(0)

        @pl.when(i == 4)
        def _():
            for w in range(ng):
                wq_copy(1, w).start()
            wo_copy(1).start()

        @pl.when(i == 5)
        def _():
            second_hop(1)
            first_hop(3)

        @pl.when(i == 7)
        def _():
            third_hop(0)

        @pl.when(i == 8)
        def _():
            second_hop(2)

        @pl.when(i == 10)
        def _():
            third_hop(1)
            first_hop(4)

        return carry

    def crop_copy(k, p):
        dev = (gy - (p % 2), (gx + 4 - p // 2) % 4, side(p, 8))
        return remote(
            nin.at[k + 1, pl.ds(64 * (3 - p), 64), :], crop.at[k, pl.ds(64 * p, 64), :],
            c_send.at[k, p - 1], c_recv.at[k, p - 1], dev,
        )

    def finish_first(k):
        for g in range(ng):
            heads_copy(k, g).wait_recv()
        for lo in (0, 2):
            rows = slice(64 * lo, 64 * lo + 128)
            own = jnp.concatenate([heads[k + 1, g, rows] for g in range(ng)], axis=1)
            oth = jnp.concatenate([heads_in[k, g, rows] for g in range(ng)], axis=1)

            def chunk(c, carry, lo=lo, rows=rows, own=own, oth=oth):
                cols = pl.ds(pl.multiple_of(c * 512, 512), 512)
                acc = jnp.dot(own, wo_own[0, :, cols], preferred_element_type=F32)
                acc = acc + jnp.dot(oth, wo_oth[0, :, cols], preferred_element_type=F32)
                acc = acc * lscale[0:1, cols]
                x[k + 1, lo : lo + 2, :, :, cols] += acc.reshape(2, 8, 8, 512)
                if k == 0:
                    fin_out[rows, cols] = acc.astype(BF)
                return carry

            lax.fori_loop(0, dim // 512, chunk, 0)
            norm_into(k + 1, 1, (lo, lo + 1))
            if lo == 0:
                crop_copy(k, 2).start()

                @pl.when(gy > 0)
                def _():
                    crop_copy(k, 3).start()
            else:

                @pl.when(gy > 0)
                def _():
                    crop_copy(k, 1).start()

        crop[k, 0:64] = nin[k + 1, 192:256]

    lax.fori_loop(0, steps, first_step, 0)
    wo_copy(0).wait()
    arrived(0)
    finish_first(0)
    second_hop(3)
    third_hop(2)
    for g in range(ng):
        wq_copy(1, g).wait()
    wo_copy(1).wait()
    second_hop(4)
    finish_first(1)
    third_hop(3)

    def upd_copy(k, p):
        dev = (gy + (p % 2), (gx + p // 2) % 4, side(p, 7))
        return remote(upd_out.at[k, p - 1], upd_in.at[k, 3 - p], u_send.at[k, p - 1], u_recv.at[k, p - 1], dev)

    def fin_copy(t):
        return remote(fin_out.at[pl.ds(64 * t, 64), :], fin_in.at[t], f_send.at[t], f_recv.at[t], mate)

    def crop_ready(k):
        crop_copy(k, 2).wait_recv()

        @pl.when(gy < 15)
        def _():
            crop_copy(k, 1).wait_recv()
            crop_copy(k, 3).wait_recv()

    def attend_crop(k):
        crop_ready(k)
        keep(project_in(crop[k], ng))

        def step(g, carry):
            if k == 0:

                @pl.when(g == 2)
                def _():
                    arrived(1)

                @pl.when(g == 3)
                def _():
                    finish_first(2)
                    third_hop(4)
                    arrived(2)

                @pl.when(g == 4)
                def _():
                    arrived(3)

            parts = project_in(crop[k], ng + g + 1)
            heads2[g] = attend(qkv[0], qkv[1], qkv[2], bias[1, 0:1, :])
            keep(parts)
            return carry

        lax.fori_loop(0, 2 * ng - 1, step, 0)
        heads2[2 * ng - 1] = attend(qkv[0], qkv[1], qkv[2], bias[1, 0:1, :])

    def project_crop(k):
        for lo in (128, 0):
            own = jnp.concatenate([heads2[g, lo : lo + 128] for g in range(ng)], axis=1)
            oth = jnp.concatenate([heads2[ng + g, lo : lo + 128] for g in range(ng)], axis=1)

            def chunk(c, carry, lo=lo, own=own, oth=oth):
                cols = pl.ds(pl.multiple_of(c * 512, 512), 512)
                acc = jnp.dot(own, wo_own[1, :, cols], preferred_element_type=F32)
                acc = acc + jnp.dot(oth, wo_oth[1, :, cols], preferred_element_type=F32)
                weight = jnp.concatenate([blend[lo : lo + 128]] * 4, axis=1)
                acc = acc * (lscale[1:2, cols] * weight)
                if lo == 0:
                    x[k + 1, 3, :, :, cols] += acc[:64].reshape(8, 8, 512)
                    upd_out[k, 0, :, cols] = acc[64:].astype(BF)
                    if k == 0:
                        fin_out[192:256, cols] = (fin_out[192:256, cols].astype(F32) + acc[:64]).astype(BF)
                else:
                    upd_out[k, 1, :, cols] = acc[:64].astype(BF)
                    upd_out[k, 2, :, cols] = acc[64:].astype(BF)
                return carry

            lax.fori_loop(0, dim // 512, chunk, 0)
            if lo == 128:
                upd_copy(k, 2).start()

                @pl.when(gy < 15)
                def _():
                    upd_copy(k, 3).start()
            else:

                @pl.when(gy < 15)
                def _():
                    upd_copy(k, 1).start()

                if k == 0:
                    fin_copy(3).start()

    def blend_in(k):
        upd_copy(k, 2).wait_recv()

        @pl.when(gy > 0)
        def _():
            upd_copy(k, 1).wait_recv()
            upd_copy(k, 3).wait_recv()

        for t in (0, 1, 2):
            come = upd_in[k, t].astype(F32)
            if t < 2:
                come = jnp.where(gx > 0, come, 0.0)
            x[k + 1, t] += come.reshape(8, 8, dim)
            if k == 0:
                rows = slice(64 * t, 64 * t + 64)
                fin_out[rows] = (fin_out[rows].astype(F32) + come).astype(BF)
                fin_copy(t).start()

    attend_crop(0)
    arrived(4)
    project_crop(0)
    attend_crop(1)
    project_crop(1)
    blend_in(0)
    attend_crop(2)
    project_crop(2)
    blend_in(1)
    for t in (3, 0, 1, 2):
        fin_copy(t).wait_recv()
        x[0, t] += fin_in[t].astype(F32).reshape(8, 8, dim)
    blend_in(2)

    for s in range(len(STAGES)):
        for c in x_copies(s):
            c.wait_send()
        for c in n_copies(s):
            c.wait_send()
        for i in range(4):
            b_copy(s, i).wait_send()
    for k in range(3):
        for g in range(ng):
            heads_copy(k, g).wait_send()
        crop_copy(k, 2).wait_send()
        upd_copy(k, 2).wait_send()

        @pl.when(gy > 0)
        def _():
            crop_copy(k, 1).wait_send()
            crop_copy(k, 3).wait_send()

        @pl.when(gy < 15)
        def _():
            upd_copy(k, 1).wait_send()
            upd_copy(k, 3).wait_send()

    for t in range(4):
        fin_copy(t).wait_send()


def blend_rows():
    token = np.arange(256)
    t, rr, cc = token // 64, (token % 64) // 8, token % 8
    r, c = 8 * (t % 2) + rr, 8 * (t // 2) + cc
    row = np.sin(np.pi * (r.astype(np.float32) + 0.5) / 16) ** 2
    col = np.sin(np.pi * (c.astype(np.float32) + 0.5) / 16) ** 2
    weight = (0.25 + 0.75 * row * col).astype(np.float32)
    return np.broadcast_to(weight[:, None], (256, 128)).copy()


def copy_kernel(src, dst, sems):
    images = images_of(lax.axis_index("gy"), lax.axis_index("tp"))
    parts = [
        pltpu.make_async_copy(src.at[slot, t], quad(dst, images[slot], t), sems.at[slot, t])
        for slot in range(4)
        for t in range(4)
    ]
    for c in parts:
        c.start()
    for c in parts:
        c.wait()


def shards(features, qkv_weight, out_weight, norm_gain, layer_scale, valid_counts):
    dim = features.shape[-1]
    half = out_weight.shape[1]
    ng = half // 256
    anywhere = pl.BlockSpec(memory_space=pl.ANY)
    vmem = pl.BlockSpec(memory_space=pltpu.VMEM)
    dma = pltpu.SemaphoreType.DMA
    ns = len(STAGES)
    result = pl.pallas_call(
        kernel,
        out_shape=pltpu.VMEM((4, 4, 8, 8, dim), F32),
        in_specs=[pl.BlockSpec(memory_space=pltpu.SMEM), anywhere, anywhere, anywhere, vmem, vmem, vmem],
        out_specs=vmem,
        scratch_shapes=[
            pltpu.VMEM((3 * ng, 3, dim, 256), BF),
            pltpu.VMEM((2, half, dim), BF),
            pltpu.VMEM((2, half, dim), BF),
            pltpu.VMEM((4, 256, dim), BF),
            pltpu.VMEM((3, 256, dim), BF),
            pltpu.VMEM((3, 256, 256), BF),
            pltpu.VMEM((4, ng, 256, 256), BF),
            pltpu.VMEM((3, ng, 256, 256), BF),
            pltpu.VMEM((2 * ng, 256, 256), BF),
            pltpu.VMEM((3, 3, 64, dim), BF),
            pltpu.VMEM((3, 3, 64, dim), BF),
            pltpu.VMEM((256, dim), BF),
            pltpu.VMEM((4, 64, dim), BF),
            pltpu.VMEM((2, 8, 256), F32),
            dma((4, 4)), dma((2 * ng,)), dma((2,)),
            dma((3, ng)), dma((3, ng)), dma((3, 3)), dma((3, 3)), dma((3, 3)), dma((3, 3)), dma((4,)), dma((4,)),
            dma((ns, 2)), dma((ns, 2)), dma((ns, 4)), dma((ns, 4)), dma((ns, 4)), dma((ns, 4)),
        ],
        compiler_params=pltpu.CompilerParams(
            collective_id=0, has_side_effects=True, vmem_limit_bytes=54 * 2**20
        ),
        name="two_sublayers",
    )(
        valid_counts.T, features, jnp.transpose(qkv_weight, (0, 2, 1, 3)), out_weight,
        norm_gain, layer_scale, jnp.asarray(blend_rows()),
    )
    return pl.pallas_call(
        copy_kernel,
        out_shape=jax.ShapeDtypeStruct(features.shape, F32),
        in_specs=[vmem],
        out_specs=anywhere,
        scratch_shapes=[dma((4, 4))],
        compiler_params=pltpu.CompilerParams(vmem_limit_bytes=16 * 2**20),
        name="result",
    )(result)


def solution(mesh):
    in_specs = (
        P(None, "gy", "gx", None),
        P(None, None, None, "tp"),
        P(None, "tp", None),
        P(),
        P(),
        P(),
    )
    out_specs = P(None, "gy", "gx", None)
    return jax.shard_map(shards, mesh=mesh, in_specs=in_specs, out_specs=out_specs, check_vma=False)
```
